128 devices in a mesh: blk: 8 (over z_lo, x), cd: 16 (over y, z_hi, core).
Axes of the slice: x: 4, y: 4, z: 4 (z_hi: 2, z_lo: 2; z = z_hi * 2 + z_lo), core: 2. Of those that a mesh axis runs over, the one named last changes fastest.
Arguments:
- integrals: float32 [256, 589824], P('blk', 'cd'), may hold values from -0.0078125 to 0.0078125
- tau: float32 [1024, 589824], P('blk', 'cd'), may hold values from -6 to 6
- singles: float32 [128, 768], replicated, may hold values from -0.5 to 0.5
- doubles: float32 [1024, 2, 768], P('blk', None, 'cd'), may hold values from -6 to 6
Outputs:
- updated: float32 [1024, 2, 768], P('blk', None, 'cd')
The draws below stay inside these ranges and needn't reach their ends.
All inputs are finite; a program needn't handle non-finite values.
Results may differ from the reference program's by a relative error of at most 0.000088.
Values sent between devices are 32-bit elements; how exact they have to be, the bound alone decides.
A program may use at most 128 MiB of HBM per device.

```python
import jax
import jax.numpy as jnp
from jax import lax

O = 128
V = 768
OT = 8
A_WIN = 2
PAIR_DEV = 128
PAIRS = 1024
KA = 256
CDP = 589824
N_BLK = 8


def block_scale(own_key, shape, shards, least, high):
    factor_of, own = 1.0, jax.random.fold_in(own_key, 6)
    for axis_at, blocks in shards:
        steps = jnp.exp(jax.random.uniform(jax.random.fold_in(own, axis_at), (blocks,), jnp.float32, least / len(shards), high / len(shards)))
        factor_of = factor_of * jnp.repeat(steps, shape[axis_at] // blocks).reshape([-1 if axis == axis_at else 1 for axis in range(len(shape))])
    return factor_of


def centred(stream_key, dims, scale, limit, pieces=(), dtype=jnp.bfloat16):
    entries = jax.random.normal(stream_key, dims, jnp.float32) * scale
    if len(pieces) > 0:
        entries = block_scale(stream_key, dims, pieces, -0.22, 0.18) * entries
    return jnp.clip(entries, min=-limit, max=limit).astype(dtype)


def setup_inputs(seed: int = 0) -> dict:
    key_of = jax.random.split(jax.random.key(seed), 5)
    return {
        "integrals": centred(key_of[0], (KA, CDP), (V * V) ** -0.5, 0.0078125, ((0, 8), (1, 16)), jnp.float32),
        "tau": centred(key_of[1], (PAIRS, CDP), 1.0, 6.0, ((0, 8), (1, 16)), jnp.float32),
        "singles": centred(key_of[2], (O, V), O ** -0.5, 0.5, (), jnp.float32),
        "doubles": centred(key_of[3], (PAIRS, A_WIN, V), 1.0, 6.0, ((0, 8), (2, 16)), jnp.float32),
    }


def reference(integrals, tau, singles, doubles):
    tiles = tau.reshape(N_BLK, PAIR_DEV, CDP)

    def one_tile(block):
        zeta = lax.dot_general(block, integrals, (((1,), (1,)), ((), ())), precision=lax.Precision.HIGHEST, preferred_element_type=jnp.float32)
        zeta = zeta.reshape(PAIR_DEV, A_WIN, O)
        folded = jnp.einsum("pak,kb->pab", zeta, singles, precision=lax.Precision.HIGHEST)
        shaped = folded.reshape(2, OT, OT, A_WIN, V)
        swapped = jnp.transpose(shaped[::-1], (0, 2, 1, 3, 4)).reshape(PAIR_DEV, A_WIN, V)
        return folded + swapped

    terms = lax.map(one_tile, tiles).reshape(PAIRS, A_WIN, V)
    return doubles - terms
```

```python
import jax
import jax.numpy as jnp
from jax import lax
from jax.experimental import pallas as pl
from jax.experimental.pallas import tpu as pltpu
from jax.sharding import PartitionSpec as P

MESH = pl.DeviceIdType.MESH
N_BLK, N_CD = 8, 16
ROWS, KA = 64, 32
JA, JB = 6, 3
OTHERS = ((1, 2), (0, 2), (0, 1))


def corner(b):
    x = b % 4
    return (((x + 1) // 2) % 2, x // 2, b // 4)


def block_of(v):
    return v[2] * 4 + v[1] * 2 + (v[0] + v[1]) % 2


def flipped(v, dims):
    return tuple((e + 1) % 2 if at in dims else e for at, e in enumerate(v))


def masked(v, d, m):
    return flipped(v, [o for bit, o in enumerate(OTHERS[d]) if (m >> bit) & 1])


def spot(v, d):
    return v[OTHERS[d][0]] + 2 * v[OTHERS[d][1]]


def tile_at(v, d, slot):
    new = list(v)
    new[OTHERS[d][0]] = slot % 2
    new[OTHERS[d][1]] = slot // 2
    return block_of(new)


def halves(x):
    high = x.astype(jnp.bfloat16)
    return high, (x - high.astype(jnp.float32)).astype(jnp.bfloat16)


def product(a, b, dims):
    a_high, a_low = halves(a)
    b_high, b_low = halves(b)

    def dot(l, r):
        return lax.dot_general(l, r, (dims, ((), ())), preferred_element_type=jnp.float32)

    return dot(a_high, b_high) + (dot(a_high, b_low) + dot(a_low, b_high))


def kernel(
    tau, integrals, singles, out,
    stage, sent, pairs, slabs, zeta, parts, summed, tiles, whole, columns, folded,
    stage_sem, own_sem, a_send, a_recv, b_send, b_recv, f_send, f_recv,
    s1, r1, s2, r2, s3, r3,
):
    b, c = lax.axis_index("blk"), lax.axis_index("cd")
    v = corner(b)
    depth = integrals.shape[1] // 12
    ka, kb = depth // JA, depth // JB
    width = singles.shape[1] // N_CD

    def base(d, m):
        return (d * 4 + spot(masked(v, d, m), d)) * depth

    def load(step, slot):
        j, d = step // 3, step % 3
        return [
            pltpu.make_async_copy(
                tau.at[:, pl.ds(pl.multiple_of(load_base(d, m) + j * ka, 128), ka)],
                stage.at[slot, m],
                stage_sem.at[slot, m],
            )
            for m in range(4)
        ]

    def load_base(d, m):
        if isinstance(d, int):
            return base(d, m)
        return jnp.where(d == 0, base(0, m), jnp.where(d == 1, base(1, m), base(2, m)))

    for copy in load(0, 0):
        copy.start()

    barrier = pltpu.get_barrier_semaphore()
    for o in range(1, N_BLK):
        pl.semaphore_signal(barrier, inc=1, device_id=((b + o) % N_BLK, c), device_id_type=MESH)
    for o in range(1, N_CD):
        pl.semaphore_signal(barrier, inc=1, device_id=(b, (c + o) % N_CD), device_id_type=MESH)
    pl.semaphore_wait(barrier, N_BLK + N_CD - 2)

    def b_copy(d, j, m):
        return pltpu.make_async_remote_copy(
            src_ref=integrals.at[:, pl.ds(pl.multiple_of(base(d, m) + j * kb, 128), kb)],
            dst_ref=slabs.at[d, j, b],
            send_sem=b_send.at[d, j, m],
            recv_sem=b_recv.at[d, j, m],
            device_id=(block_of(masked(v, d, m)), c),
            device_id_type=MESH,
        )

    def b_own(d, j):
        return pltpu.make_async_copy(
            integrals.at[:, pl.ds(pl.multiple_of(base(d, 0) + j * kb, 128), kb)], slabs.at[d, j, b], own_sem.at[d, j]
        )

    def f_copy(d, j, m):
        block = slabs.at[d, j, block_of(masked(v, d, m))]
        return pltpu.make_async_remote_copy(
            src_ref=block,
            dst_ref=block,
            send_sem=f_send.at[d, j, m],
            recv_sem=f_recv.at[d, j, m],
            device_id=(block_of(flipped(v, [d])), c),
            device_id_type=MESH,
        )

    def f_arrival(d, j, m):
        block = slabs.at[d, j, block_of(flipped(masked(v, d, m), [d]))]
        return pltpu.make_async_remote_copy(
            src_ref=block,
            dst_ref=block,
            send_sem=f_send.at[d, j, m],
            recv_sem=f_recv.at[d, j, m],
            device_id=(block_of(flipped(v, [d])), c),
            device_id_type=MESH,
        )

    def a_copy(d, j, m):
        return pltpu.make_async_remote_copy(
            src_ref=sent.at[d, j, m - 1],
            dst_ref=pairs.at[d, j, spot(v, d)],
            send_sem=a_send.at[d, j, m],
            recv_sem=a_recv.at[d, j, m],
            device_id=(block_of(masked(v, d, m)), c),
            device_id_type=MESH,
        )

    def b_start(j, carry):
        for d in range(3):
            b_own(d, j).start()
            for m in range(1, 4):
                b_copy(d, j, m).start()
        return carry

    lax.fori_loop(0, JB, b_start, 0)

    def add_pairs(slot, m, put):
        back = stage[slot, m, pl.ds(ROWS, ROWS), :].reshape(8, 8, ka)
        back = jnp.swapaxes(back, 0, 1).reshape(ROWS, ka)
        put(stage[slot, m, pl.ds(0, ROWS), :] + back)

    def a_start(j, carry):
        for d in range(3):
            step = j * 3 + d
            slot = step % 2
            for copy in load(step, slot):
                copy.wait()
            if d < 2:
                for copy in load(step + 1, (step + 1) % 2):
                    copy.start()
            else:

                @pl.when(j < JA - 1)
                def _():
                    for copy in load(step + 1, (step + 1) % 2):
                        copy.start()

            for m in range(1, 4):

                def put(value):
                    sent[d, j, m - 1] = value

                add_pairs(slot, m, put)
                a_copy(d, j, m).start()

            def put_own(value):
                pairs[d, j, spot(v, d)] = value

            add_pairs(slot, 0, put_own)
        return carry

    lax.fori_loop(0, JA, a_start, 0)

    def forward(j, carry):
        for d in range(3):
            b_own(d, j).wait()
            f_copy(d, j, 0).start()
            for m in range(1, 4):
                b_copy(d, j, m).wait_recv()
                f_copy(d, j, m).start()
        return carry

    lax.fori_loop(0, JB, forward, 0)

    zeta[...] = jnp.zeros_like(zeta)
    columns[...] = pltpu.roll(singles[...], (N_CD - c) % N_CD * width, 1)[:, :128]

    def multiply(jb, carry):
        for d in range(3):
            for m in range(4):
                f_arrival(d, jb, m).wait_recv()
        for ja in range(JA // JB):
            j = jb * (JA // JB) + ja
            for d in range(3):
                for m in range(1, 4):
                    a_copy(d, j, m).wait_recv()
                left = pairs[d, j].reshape(4 * ROWS, ka)
                right = slabs[d, jb, :, :, pl.ds(ja * ka, ka)].reshape(N_BLK * KA, ka)
                part = product(left, right, ((1,), (1,)))
                for slot in range(4):
                    t = tile_at(v, d, slot)
                    rows = part[slot * ROWS : (slot + 1) * ROWS]
                    zeta[0, t] += rows[:, :128]
                    zeta[1, t] += rows[:, 128:]
        return carry

    lax.fori_loop(0, JB, multiply, 0)

    def to_cd(o):
        peer = (c + o) % N_CD
        return pltpu.make_async_remote_copy(
            src_ref=zeta.at[peer % 2, :, pl.ds(pl.multiple_of(peer // 2 * 8, 8), 8), :],
            dst_ref=parts.at[o],
            send_sem=s1.at[o],
            recv_sem=r1.at[o],
            device_id=(b, peer),
            device_id_type=MESH,
        )

    def to_tile(o):
        peer = (b + o) % N_BLK
        return pltpu.make_async_remote_copy(
            src_ref=summed.at[peer],
            dst_ref=tiles.at[o],
            send_sem=s2.at[o],
            recv_sem=r2.at[o],
            device_id=(peer, c),
            device_id_type=MESH,
        )

    def to_all(o):
        return pltpu.make_async_remote_copy(
            src_ref=whole.at[c % 2, c // 2],
            dst_ref=whole.at[c % 2, c // 2],
            send_sem=s3.at[o],
            recv_sem=r3.at[o],
            device_id=(b, (c + o) % N_CD),
            device_id_type=MESH,
        )

    def from_all(o):
        peer = (c + N_CD - o) % N_CD
        return pltpu.make_async_remote_copy(
            src_ref=whole.at[peer % 2, peer // 2],
            dst_ref=whole.at[peer % 2, peer // 2],
            send_sem=s3.at[o],
            recv_sem=r3.at[o],
            device_id=(b, (c + o) % N_CD),
            device_id_type=MESH,
        )

    for o in range(1, N_CD):
        to_cd(o).start()
    total = zeta[c % 2, :, pl.ds(pl.multiple_of(c // 2 * 8, 8), 8), :]
    for o in range(1, N_CD):
        to_cd(o).wait_recv()
        total = total + parts[o]
    summed[...] = total

    for o in range(1, N_BLK):
        to_tile(o).start()
    mine = summed[b]
    for o in range(1, N_BLK):
        to_tile(o).wait_recv()
        mine = mine + tiles[o]
    whole[c % 2, c // 2] = mine

    for o in range(1, N_CD):
        to_all(o).start()
    for o in range(1, N_CD):
        from_all(o).wait_recv()

    for a in range(2):
        folded[...] = product(whole[a].reshape(ROWS, 128), columns[...], ((1,), (0,)))
        out[a, pl.ds(0, ROWS), :] = folded[...]
        for i in range(8):
            out[a, pl.ds(ROWS + i * 8, 8), :] = folded[pl.ds(i, 8, stride=8), :]

    def drain_b(j, carry):
        for d in range(3):
            f_copy(d, j, 0).wait_send()
            for m in range(1, 4):
                b_copy(d, j, m).wait_send()
                f_copy(d, j, m).wait_send()
        return carry

    def drain_a(j, carry):
        for d in range(3):
            for m in range(1, 4):
                a_copy(d, j, m).wait_send()
        return carry

    lax.fori_loop(0, JB, drain_b, 0)
    lax.fori_loop(0, JA, drain_a, 0)
    for o in range(1, N_CD):
        to_cd(o).wait_send()
        to_all(o).wait_send()
    for o in range(1, N_BLK):
        to_tile(o).wait_send()


def on_device(integrals, tau, singles, doubles):
    depth = integrals.shape[1] // 12
    ka, kb = depth // JA, depth // JB
    width = doubles.shape[2]
    vmem, dma, f32 = pltpu.VMEM, pltpu.SemaphoreType.DMA, jnp.float32
    any_ref, vmem_ref = pl.BlockSpec(memory_space=pl.ANY), pl.BlockSpec(memory_space=vmem)
    folded = pl.pallas_call(
        kernel,
        out_shape=jax.ShapeDtypeStruct((2, 2 * ROWS, 128), f32),
        in_specs=[any_ref, any_ref, vmem_ref],
        out_specs=vmem_ref,
        scratch_shapes=[
            vmem((2, 4, 2 * ROWS, ka), f32),
            vmem((3, JA, 3, ROWS, ka), f32),
            vmem((3, JA, 4, ROWS, ka), f32),
            vmem((3, JB, N_BLK, KA, kb), f32),
            vmem((2, N_BLK, ROWS, 128), f32),
            vmem((N_CD, N_BLK, 8, 128), f32),
            vmem((N_BLK, 8, 128), f32),
            vmem((N_BLK, 8, 128), f32),
            vmem((2, 8, 8, 128), f32),
            vmem((128, 128), f32),
            vmem((ROWS, 128), f32),
            dma((2, 4)), dma((3, JB)),
            dma((3, JA, 4)), dma((3, JA, 4)),
            dma((3, JB, 4)), dma((3, JB, 4)), dma((3, JB, 4)), dma((3, JB, 4)),
            dma((N_CD,)), dma((N_CD,)), dma((N_BLK,)), dma((N_BLK,)), dma((N_CD,)), dma((N_CD,)),
        ],
        compiler_params=pltpu.CompilerParams(
            collective_id=0, has_side_effects=True, vmem_limit_bytes=48 * 2**20
        ),
        cost_estimate=pl.CostEstimate(flops=2 * 3 * 256 * 256 * depth * 3, bytes_accessed=24 * 2**20, transcendentals=0),
    )(tau, integrals, singles)
    return doubles - jnp.transpose(folded, (1, 0, 2))[:, :, :width]


def solution(mesh):
    placed = (P("blk", "cd"), P("blk", "cd"), P(), P("blk", None, "cd"))
    return jax.shard_map(
        on_device, mesh=mesh, in_specs=placed, out_specs=P("blk", None, "cd"), check_vma=False
    )
```

```python
import jax
import jax.numpy as jnp
from jax import lax
from jax.experimental import pallas as pl
from jax.experimental.pallas import tpu as pltpu
from jax.sharding import PartitionSpec as P

MESH = pl.DeviceIdType.MESH
N_BLK, N_CD = 8, 16
ROWS, KA = 64, 32
LATE = 8
EARLY = ROWS - LATE
STEPS = 6
LATE_STEPS = 3
PER_LATE = STEPS // LATE_STEPS
OTHERS = ((1, 2), (0, 2), (0, 1))
ORDER = ((0, 1), (1, 2), (2, 1), (1, 1), (2, 2), (0, 2), (0, 3), (2, 3), (1, 3))


def corner(b):
    x = b % 4
    return (((x + 1) // 2) % 2, x // 2, b // 4)


def block_of(v):
    return v[2] * 4 + v[1] * 2 + (v[0] + v[1]) % 2


def flipped(v, dims):
    return tuple((e + 1) % 2 if at in dims else e for at, e in enumerate(v))


def masked(v, d, m):
    return flipped(v, [o for bit, o in enumerate(OTHERS[d]) if (m >> bit) & 1])


def spot(v, d):
    return v[OTHERS[d][0]] + 2 * v[OTHERS[d][1]]


def tile_at(v, d, slot):
    new = list(v)
    new[OTHERS[d][0]] = slot % 2
    new[OTHERS[d][1]] = slot // 2
    return block_of(new)


def halves(x):
    high = x.astype(jnp.bfloat16)
    return high, (x - high.astype(jnp.float32)).astype(jnp.bfloat16)


def product(a, b):
    def dot(l, r):
        return lax.dot_general(l, r, (((1,), (1,)), ((), ())), preferred_element_type=jnp.float32)

    return dot(a[0], b[0]) + (dot(a[0], b[1]) + dot(a[1], b[0]))


def arrive(ref, sem):
    pltpu.make_async_copy(ref, ref, sem).wait()


def kernel(
    tau, integrals, singles, out,
    stage, early, late, slabs, high, low, zeta, zeta_late,
    parts, summed, pieces, whole, tiles, spreads, factors, columns, spread,
    load_sem, own_sem, factor_sem, a_send, early_recv, late_recv, b_send, b_recv, f_recv, t_send, t_recv,
):
    b, c = lax.axis_index("blk"), lax.axis_index("cd")
    v = corner(b)
    depth = integrals.shape[1] // 12
    ka = depth // STEPS
    width = singles.shape[1] // N_CD
    zh, yc = c // 2 % 2, c // 4 * 2 + c % 2

    def cd_of(zh, yc):
        return yc // 2 * 4 + zh * 2 + yc % 2

    def span(d, j, m):
        return pl.ds(pl.multiple_of((d * 4 + spot(masked(v, d, m), d)) * depth + j * ka, 128), ka)

    def send(src, dst, sent, got, blk, cd):
        pltpu.make_async_remote_copy(
            src_ref=src, dst_ref=dst, send_sem=sent, recv_sem=got, device_id=(blk, cd), device_id_type=MESH
        ).start()

    def load_start(j, carry):
        for d in range(3):
            for m in range(4):
                pltpu.make_async_copy(tau.at[:, span(d, j, m)], stage.at[j, d, m], load_sem.at[j]).start()
        return carry

    lax.fori_loop(0, STEPS, load_start, 0)
    factor_copy = pltpu.make_async_copy(singles, factors, factor_sem)
    factor_copy.start()

    def own_start(j, carry):
        for d in range(3):
            pltpu.make_async_copy(integrals.at[:, span(d, j, 0)], slabs.at[j, d, b], own_sem).start()
        return carry

    lax.fori_loop(0, STEPS, own_start, 0)

    barrier = pltpu.get_barrier_semaphore()
    for o in range(1, N_BLK):
        pl.semaphore_signal(barrier, inc=1, device_id=((b + o) % N_BLK, c), device_id_type=MESH)
    for o in range(1, N_CD):
        pl.semaphore_signal(barrier, inc=1, device_id=(b, (c + o) % N_CD), device_id_type=MESH)
    pl.semaphore_wait(barrier, N_BLK + N_CD - 2)

    def b_start(j, carry):
        for d, m in ORDER:
            send(
                integrals.at[:, span(d, j, m)], slabs.at[j, d, b], b_send, b_recv.at[j], block_of(masked(v, d, m)), c
            )
        return carry

    lax.fori_loop(0, STEPS, b_start, 0)

    def pair_sums(j, d, m):
        back = stage[j, d, m, pl.ds(ROWS, ROWS), :].reshape(8, 8, ka)
        back = jnp.swapaxes(back, 0, 1).reshape(ROWS, ka)
        return stage[j, d, m, pl.ds(0, ROWS), :] + back

    def early_start(j, carry):
        arrive(stage.at[j], load_sem.at[j])
        for d, m in ORDER:
            stage[j, d, m, pl.ds(0, ROWS), :] = pair_sums(j, d, m)
            send(
                stage.at[j, d, m, pl.ds(0, EARLY), :], early.at[j, d, spot(v, d)],
                a_send, early_recv.at[j, d], block_of(masked(v, d, m)), c,
            )
        for d in range(3):
            sums = pair_sums(j, d, 0)
            early[j, d, spot(v, d)] = sums[:EARLY]
            late[j, d, spot(v, d)] = sums[EARLY:]
        return carry

    lax.fori_loop(0, STEPS, early_start, 0)

    arrive(slabs.at[:, :, 0], own_sem)

    def forward(j, carry):
        arrive(slabs.at[j, :, pl.ds(0, 3)], b_recv.at[j])
        for m in range(4):
            for d in range(3):
                block = slabs.at[j, d, block_of(masked(v, d, m))]
                send(block, block, b_send, f_recv.at[j], block_of(flipped(v, [d])), c)
        return carry

    lax.fori_loop(0, STEPS, forward, 0)

    def late_start(n, carry):
        steps = pl.ds(n * PER_LATE, PER_LATE)
        for d, m in ORDER:
            send(
                stage.at[steps, d, m, pl.ds(EARLY, LATE), :], late.at[steps, d, spot(v, d)],
                a_send, late_recv.at[n, d], block_of(masked(v, d, m)), c,
            )
        return carry

    lax.fori_loop(0, LATE_STEPS, late_start, 0)

    zeta[...] = jnp.zeros_like(zeta)
    zeta_late[...] = jnp.zeros_like(zeta_late)
    factor_copy.wait()
    columns[...] = pltpu.roll(factors[...], (N_CD - c) % N_CD * width, 1)[:, :128].T

    def multiply_early(j, carry):
        arrive(slabs.at[j, :, pl.ds(0, 4)], f_recv.at[j])
        for d in range(3):
            right = halves(slabs[j, d].reshape(N_BLK * KA, ka))
            high[j, d], low[j, d] = right
            arrive(early.at[j, d, pl.ds(0, 3)], early_recv.at[j, d])
            part = product(halves(early[j, d].reshape(4 * EARLY, ka)), right)
            for slot in range(4):
                t = tile_at(v, d, slot)
                rows = part[slot * EARLY : (slot + 1) * EARLY]
                for a in range(2):
                    zeta[t, a, pl.ds(0, EARLY // 8)] += rows[:, a * 128 : (a + 1) * 128].reshape(EARLY // 8, 8, 128)
        return carry

    lax.fori_loop(0, STEPS, multiply_early, 0)

    for o in range(1, 8):
        peer = (yc + o) % 8
        share = zeta.at[:, peer // 4, pl.ds(peer % 4 * 2, 2)]
        send(share, parts.at[o], t_send.at[0], t_recv.at[0], b, cd_of(zh, peer))

    def multiply_late(n, carry):
        for d in range(3):
            arrive(late.at[pl.ds(0, PER_LATE), d, pl.ds(0, 3)], late_recv.at[n, d])
            for s in range(PER_LATE):
                j = n * PER_LATE + s
                part = product(halves(late[j, d].reshape(4 * LATE, ka)), (high[j, d], low[j, d]))
                for slot in range(4):
                    t = tile_at(v, d, slot)
                    rows = part[slot * LATE : (slot + 1) * LATE]
                    for a in range(2):
                        zeta_late[t, a] += rows[:, a * 128 : (a + 1) * 128]
        return carry

    lax.fori_loop(0, LATE_STEPS - 1, multiply_late, 0)

    arrive(parts.at[pl.ds(1, 7)], t_recv.at[0])
    total = zeta[:, yc // 4, pl.ds(yc % 4 * 2, 2)]
    for o in range(1, 8):
        total = total + parts[o]
    summed[...] = total
    for o in range(1, N_BLK):
        peer = (b + o) % N_BLK
        send(summed.at[peer], pieces.at[o], t_send.at[1], t_recv.at[1], peer, c)

    multiply_late(LATE_STEPS - 1, 0)

    for o in range(1, N_BLK):
        peer = (b + o) % N_BLK
        send(zeta_late.at[peer], tiles.at[o], t_send.at[3], t_recv.at[3], peer, c)

    arrive(pieces.at[pl.ds(1, 7)], t_recv.at[1])
    mine = summed[b]
    for o in range(1, N_BLK):
        mine = mine + pieces[o]
    whole[c] = mine
    for o in range(1, N_CD):
        send(whole.at[c], whole.at[c], t_send.at[2], t_recv.at[2], b, (c + o) % N_CD)

    arrive(tiles.at[pl.ds(1, 7)], t_recv.at[3])
    last = zeta_late[b]
    for o in range(1, N_BLK):
        last = last + tiles[o]
    spreads[c] = last
    for o in range(1, N_CD):
        send(spreads.at[c], spreads.at[c], t_send.at[4], t_recv.at[4], b, (c + o) % N_CD)

    arrive(whole.at[pl.ds(1, 15)], t_recv.at[2])
    for a in range(2):
        for i in range(7):
            rows = whole[cd_of(0, a * 4 + i // 2), i % 2] + whole[cd_of(1, a * 4 + i // 2), i % 2]
            spread[a, pl.ds(i * 8, 8), :] = rows
            spread[a, pl.ds(ROWS + i, 8, stride=8), :] = rows

    arrive(spreads.at[pl.ds(1, 15)], t_recv.at[4])
    last = spreads[0]
    for o in range(1, N_CD):
        last = last + spreads[o]
    left = halves(columns[pl.ds(0, width), :])
    for a in range(2):
        spread[a, pl.ds(EARLY, 8), :] = last[a]
        spread[a, pl.ds(ROWS + 7, 8, stride=8), :] = last[a]
        out[a] = product(left, halves(spread[a]))

    arrive(slabs.at[:, :, pl.ds(0, 7)], b_send)
    arrive(early.at[:, :, pl.ds(0, 3)], a_send)
    arrive(late.at[:, :, pl.ds(0, 3)], a_send)
    arrive(parts.at[pl.ds(1, 7)], t_send.at[0])
    arrive(pieces.at[pl.ds(1, 7)], t_send.at[1])
    arrive(whole.at[pl.ds(1, 15)], t_send.at[2])
    arrive(tiles.at[pl.ds(1, 7)], t_send.at[3])
    arrive(spreads.at[pl.ds(1, 15)], t_send.at[4])


def on_device(integrals, tau, singles, doubles):
    depth = integrals.shape[1] // 12
    ka = depth // STEPS
    width = doubles.shape[2]
    vmem, dma, f32 = pltpu.VMEM, pltpu.SemaphoreType.DMA, jnp.float32
    any_ref, vmem_ref = pl.BlockSpec(memory_space=pl.ANY), pl.BlockSpec(memory_space=vmem)
    folded = pl.pallas_call(
        kernel,
        out_shape=jax.ShapeDtypeStruct((2, width, 2 * ROWS), f32),
        in_specs=[any_ref, any_ref, any_ref],
        out_specs=vmem_ref,
        scratch_shapes=[
            vmem((STEPS, 3, 4, 2 * ROWS, ka), f32),
            vmem((STEPS, 3, 4, EARLY, ka), f32),
            vmem((STEPS, 3, 4, LATE, ka), f32),
            vmem((STEPS, 3, N_BLK, KA, ka), f32),
            vmem((STEPS, 3, N_BLK * KA, ka), jnp.bfloat16),
            vmem((STEPS, 3, N_BLK * KA, ka), jnp.bfloat16),
            vmem((N_BLK, 2, 8, 8, 128), f32),
            vmem((N_BLK, 2, LATE, 128), f32),
            vmem((8, N_BLK, 2, 8, 128), f32),
            vmem((N_BLK, 2, 8, 128), f32),
            vmem((N_BLK, 2, 8, 128), f32),
            vmem((N_CD, 2, 8, 128), f32),
            vmem((N_BLK, 2, LATE, 128), f32),
            vmem((N_CD, 2, LATE, 128), f32),
            vmem(singles.shape, f32),
            vmem((128, 128), f32),
            vmem((2, 2 * ROWS, 128), f32),
            dma((STEPS,)), dma(()), dma(()),
            dma(()), dma((STEPS, 3)), dma((LATE_STEPS, 3)),
            dma(()), dma((STEPS,)), dma((STEPS,)),
            dma((5,)), dma((5,)),
        ],
        compiler_params=pltpu.CompilerParams(
            collective_id=0, has_side_effects=True, vmem_limit_bytes=60 * 2**20
        ),
        cost_estimate=pl.CostEstimate(flops=2 * 3 * 256 * 256 * depth * 3, bytes_accessed=24 * 2**20, transcendentals=0),
    )(tau, integrals, singles)
    return doubles - jnp.transpose(folded, (2, 0, 1))


def solution(mesh):
    placed = (P("blk", "cd"), P("blk", "cd"), P(), P("blk", None, "cd"))
    return jax.shard_map(
        on_device, mesh=mesh, in_specs=placed, out_specs=P("blk", None, "cd"), check_vma=False
    )
```

```python
import jax
import jax.numpy as jnp
from jax import lax
from jax.experimental import pallas as pl
from jax.experimental.pallas import tpu as pltpu
from jax.sharding import PartitionSpec as P

MESH = pl.DeviceIdType.MESH
N_BLK, N_CD = 8, 16
ROWS, KA = 64, 32
LATE, N_LATE = 8, 2
EARLY = ROWS - LATE * N_LATE
STEPS = 6
LATE_STEPS = (6, 6)
OTHERS = ((1, 2), (0, 2), (0, 1))
FAR_CD = (10, 11, 6, 7, 14, 15, 8, 9, 2, 3, 4, 5, 12, 13, 1)
FAR_BLK = (6, 2, 5, 7, 4, 1, 3)
ORDER = ((0, 1), (1, 2), (2, 1), (1, 1), (2, 2), (0, 2), (0, 3), (2, 3), (1, 3))


def corner(b):
    x = b % 4
    return (((x + 1) // 2) % 2, x // 2, b // 4)


def block_of(v):
    return v[2] * 4 + v[1] * 2 + (v[0] + v[1]) % 2


def flipped(v, dims):
    return tuple((e + 1) % 2 if at in dims else e for at, e in enumerate(v))


def masked(v, d, m):
    return flipped(v, [o for bit, o in enumerate(OTHERS[d]) if (m >> bit) & 1])


def spot(v, d):
    return v[OTHERS[d][0]] + 2 * v[OTHERS[d][1]]


def tile_at(v, d, slot):
    new = list(v)
    new[OTHERS[d][0]] = slot % 2
    new[OTHERS[d][1]] = slot // 2
    return block_of(new)


def halves(x):
    high = x.astype(jnp.bfloat16)
    return high, (x - high.astype(jnp.float32)).astype(jnp.bfloat16)


def product(a, b, stacked=False):
    def dot(l, r):
        return lax.dot_general(l, r, (((1,), (1,)), ((), ())), preferred_element_type=jnp.float32)

    if stacked:
        both = dot(jnp.concatenate(a), b[0])
        n = a[0].shape[0]
        return both[:n] + (dot(a[0], b[1]) + both[n:])
    return dot(a[0], b[0]) + (dot(a[0], b[1]) + dot(a[1], b[0]))


def arrive(ref, sem):
    pltpu.make_async_copy(ref, ref, sem).wait()


def kernel(
    tau, integrals, singles, out,
    stage, early, late, slabs, high, low, zeta, zeta_late,
    parts, summed, pieces, whole, tiles, spreads, factors, columns, spread,
    load_sem, own_sem, factor_sem, a_send, early_recv, late_recv, b_send, b_recv, f_recv, t_send, t_recv,
):
    b, c = lax.axis_index("blk"), lax.axis_index("cd")
    v = corner(b)
    depth = integrals.shape[1] // 12
    ka = depth // STEPS
    width = singles.shape[1] // N_CD
    zh, yc = c // 2 % 2, c // 4 * 2 + c % 2

    def cd_of(zh, yc):
        return yc // 2 * 4 + zh * 2 + yc % 2

    def cd_at(o):
        return (c // 4 + o // 4) % 4 * 4 + (c // 2 + o // 2) % 2 * 2 + (c + o) % 2

    def blk_at(o):
        return (b // 4 + o // 4) % 2 * 4 + (b + o) % 4

    def span(d, j, m):
        return pl.ds(pl.multiple_of((d * 4 + spot(masked(v, d, m), d)) * depth + j * ka, 128), ka)

    def send(src, dst, sent, got, blk, cd):
        pltpu.make_async_remote_copy(
            src_ref=src, dst_ref=dst, send_sem=sent, recv_sem=got, device_id=(blk, cd), device_id_type=MESH
        ).start()

    barrier = pltpu.get_barrier_semaphore()
    for o in FAR_CD:
        pl.semaphore_signal(barrier, inc=1, device_id=(b, cd_at(o)), device_id_type=MESH)
    for o in FAR_BLK:
        pl.semaphore_signal(barrier, inc=1, device_id=(blk_at(o), c), device_id_type=MESH)

    def load_start(j, carry):
        for d in range(3):
            for m in range(4):
                pltpu.make_async_copy(tau.at[:, span(d, j, m)], stage.at[j, d, m], load_sem.at[j]).start()
        return carry

    lax.fori_loop(0, STEPS, load_start, 0)
    factor_copy = pltpu.make_async_copy(singles, factors, factor_sem)
    factor_copy.start()

    def own_start(j, carry):
        for d in range(3):
            pltpu.make_async_copy(integrals.at[:, span(d, j, 0)], slabs.at[j, d, b], own_sem).start()
        return carry

    lax.fori_loop(0, STEPS, own_start, 0)

    pl.semaphore_wait(barrier, N_BLK + N_CD - 2)

    def b_start(j, carry):
        for d, m in ORDER:
            send(
                integrals.at[:, span(d, j, m)], slabs.at[j, d, b], b_send, b_recv.at[j], block_of(masked(v, d, m)), c
            )
        return carry

    lax.fori_loop(0, STEPS, b_start, 0)

    def pair_sums(j, d, m):
        back = stage[j, d, m, pl.ds(ROWS, ROWS), :].reshape(8, 8, ka)
        back = jnp.swapaxes(back, 0, 1).reshape(ROWS, ka)
        return stage[j, d, m, pl.ds(0, ROWS), :] + back

    def early_start(j, carry):
        arrive(stage.at[j], load_sem.at[j])
        for d, m in ORDER:
            stage[j, d, m, pl.ds(0, ROWS), :] = pair_sums(j, d, m)
            send(
                stage.at[j, d, m, pl.ds(0, EARLY), :], early.at[j, d, spot(v, d)],
                a_send, early_recv.at[j, d], block_of(masked(v, d, m)), c,
            )
        for d in range(3):
            sums = pair_sums(j, d, 0)
            early[j, d, spot(v, d)] = sums[:EARLY]
            for g in range(N_LATE):
                late[g, j, d, spot(v, d)] = sums[EARLY + g * LATE : EARLY + (g + 1) * LATE]
        return carry

    lax.fori_loop(0, STEPS, early_start, 0)

    arrive(slabs.at[:, :, 0], own_sem)

    def forward(j, carry):
        arrive(slabs.at[j, :, pl.ds(0, 3)], b_recv.at[j])
        for m in range(4):
            for d in range(3):
                block = slabs.at[j, d, block_of(masked(v, d, m))]
                send(block, block, b_send, f_recv.at[j], block_of(flipped(v, [d])), c)
        return carry

    lax.fori_loop(0, STEPS, forward, 0)

    def late_start(g):
        per = STEPS // LATE_STEPS[g]

        def start(n, carry):
            steps = pl.ds(n * per, per)
            for d, m in ORDER:
                send(
                    stage.at[steps, d, m, pl.ds(EARLY + g * LATE, LATE), :], late.at[g, steps, d, spot(v, d)],
                    a_send, late_recv.at[g, n, d], block_of(masked(v, d, m)), c,
                )
            return carry

        lax.fori_loop(0, LATE_STEPS[g], start, 0)

    for g in range(N_LATE):
        late_start(g)

    zeta[...] = jnp.zeros_like(zeta)
    zeta_late[...] = jnp.zeros_like(zeta_late)
    factor_copy.wait()
    columns[...] = pltpu.roll(factors[...], (N_CD - c) % N_CD * width, 1)[:, :128].T

    def multiply_early(j, carry):
        arrive(slabs.at[j, :, pl.ds(0, 4)], f_recv.at[j])
        for d in range(3):
            right = halves(slabs[j, d].reshape(N_BLK * KA, ka))
            high[j, d], low[j, d] = right
            arrive(early.at[j, d, pl.ds(0, 3)], early_recv.at[j, d])
            part = product(halves(early[j, d].reshape(4 * EARLY, ka)), right)
            for slot in range(4):
                t = tile_at(v, d, slot)
                rows = part[slot * EARLY : (slot + 1) * EARLY]
                for a in range(2):
                    zeta[t, a, pl.ds(0, EARLY // 8)] += rows[:, a * 128 : (a + 1) * 128].reshape(EARLY // 8, 8, 128)
        return carry

    lax.fori_loop(0, STEPS, multiply_early, 0)

    for o in (4, 5, 2, 3, 6, 7, 1):
        peer = (yc // 2 + o // 2) % 4 * 2 + (yc + o) % 2
        share = zeta.at[:, peer // 4, pl.ds(peer % 4 * 2, 2)]
        send(share, parts.at[o], t_send.at[0], t_recv.at[0], b, cd_of(zh, peer))

    def multiply_late(g, first, end):
        per = STEPS // LATE_STEPS[g]

        def multiply(n, carry):
            for d in range(3):
                arrive(late.at[g, pl.ds(0, per), d, pl.ds(0, 3)], late_recv.at[g, n, d])
                for s in range(per):
                    j = n * per + s
                    part = product(halves(late[g, j, d].reshape(4 * LATE, ka)), (high[j, d], low[j, d]), True)
                    for slot in range(4):
                        t = tile_at(v, d, slot)
                        rows = part[slot * LATE : (slot + 1) * LATE]
                        for a in range(2):
                            zeta_late[g, t, a] += rows[:, a * 128 : (a + 1) * 128]
            return carry

        lax.fori_loop(first, end, multiply, 0)

    def late_to_tiles(g):
        for o in FAR_BLK:
            peer = blk_at(o)
            send(zeta_late.at[g, peer], tiles.at[g, o], t_send.at[3 + g], t_recv.at[3 + g], peer, c)

    def late_to_all(g):
        arrive(tiles.at[g, pl.ds(1, 7)], t_recv.at[3 + g])
        last = zeta_late[g, b]
        for o in range(1, N_BLK):
            last = last + tiles[g, o]
        spreads[g, c] = last
        for o in FAR_CD:
            send(
                spreads.at[g, c], spreads.at[g, c],
                t_send.at[3 + N_LATE + g], t_recv.at[3 + N_LATE + g], b, cd_at(o),
            )

    def late_rows(g):
        arrive(spreads.at[g, pl.ds(1, 15)], t_recv.at[3 + N_LATE + g])
        last = spreads[g, 0]
        for o in range(1, N_CD):
            last = last + spreads[g, o]
        at = EARLY // 8 + g
        for a in range(2):
            spread[a, pl.ds(at * 8, 8), :] = last[a]
            spread[a, pl.ds(ROWS + at, 8, stride=8), :] = last[a]

    multiply_late(0, 0, LATE_STEPS[0])
    late_to_tiles(0)

    arrive(parts.at[pl.ds(1, 7)], t_recv.at[0])
    total = zeta[:, yc // 4, pl.ds(yc % 4 * 2, 2)]
    for o in range(1, 8):
        total = total + parts[o]
    summed[...] = total
    for o in FAR_BLK:
        peer = blk_at(o)
        send(summed.at[peer], pieces.at[o], t_send.at[1], t_recv.at[1], peer, c)

    multiply_late(1, 0, LATE_STEPS[1] - 1)
    late_to_all(0)
    multiply_late(1, LATE_STEPS[1] - 1, LATE_STEPS[1])
    late_to_tiles(1)

    arrive(pieces.at[pl.ds(1, 7)], t_recv.at[1])
    mine = summed[b]
    for o in range(1, N_BLK):
        mine = mine + pieces[o]
    whole[c] = mine
    for o in FAR_CD:
        send(whole.at[c], whole.at[c], t_send.at[2], t_recv.at[2], b, cd_at(o))

    late_to_all(1)
    arrive(whole.at[pl.ds(1, 15)], t_recv.at[2])
    for a in range(2):
        for i in range(EARLY // 8):
            rows = whole[cd_of(0, a * 4 + i // 2), i % 2] + whole[cd_of(1, a * 4 + i // 2), i % 2]
            spread[a, pl.ds(i * 8, 8), :] = rows
            spread[a, pl.ds(ROWS + i, 8, stride=8), :] = rows

    late_rows(0)
    arrive(slabs.at[:, :, pl.ds(0, 7)], b_send)
    arrive(early.at[:, :, pl.ds(0, 3)], a_send)
    arrive(late.at[:, :, :, pl.ds(0, 3)], a_send)
    arrive(parts.at[pl.ds(1, 7)], t_send.at[0])
    arrive(pieces.at[pl.ds(1, 7)], t_send.at[1])
    left = halves(columns[pl.ds(0, width), :])
    late_rows(1)
    for a in range(2):
        out[a] = product(left, halves(spread[a]))

    arrive(whole.at[pl.ds(1, 15)], t_send.at[2])
    for g in range(N_LATE):
        arrive(tiles.at[g, pl.ds(1, 7)], t_send.at[3 + g])
        arrive(spreads.at[g, pl.ds(1, 15)], t_send.at[3 + N_LATE + g])


def on_device(integrals, tau, singles, doubles):
    depth = integrals.shape[1] // 12
    ka = depth // STEPS
    width = doubles.shape[2]
    vmem, dma, f32 = pltpu.VMEM, pltpu.SemaphoreType.DMA, jnp.float32
    any_ref, vmem_ref = pl.BlockSpec(memory_space=pl.ANY), pl.BlockSpec(memory_space=vmem)
    folded = pl.pallas_call(
        kernel,
        out_shape=jax.ShapeDtypeStruct((2, width, 2 * ROWS), f32),
        in_specs=[any_ref, any_ref, any_ref],
        out_specs=vmem_ref,
        scratch_shapes=[
            vmem((STEPS, 3, 4, 2 * ROWS, ka), f32),
            vmem((STEPS, 3, 4, EARLY, ka), f32),
            vmem((N_LATE, STEPS, 3, 4, LATE, ka), f32),
            vmem((STEPS, 3, N_BLK, KA, ka), f32),
            vmem((STEPS, 3, N_BLK * KA, ka), jnp.bfloat16),
            vmem((STEPS, 3, N_BLK * KA, ka), jnp.bfloat16),
            vmem((N_BLK, 2, 8, 8, 128), f32),
            vmem((N_LATE, N_BLK, 2, LATE, 128), f32),
            vmem((8, N_BLK, 2, 8, 128), f32),
            vmem((N_BLK, 2, 8, 128), f32),
            vmem((N_BLK, 2, 8, 128), f32),
            vmem((N_CD, 2, 8, 128), f32),
            vmem((N_LATE, N_BLK, 2, LATE, 128), f32),
            vmem((N_LATE, N_CD, 2, LATE, 128), f32),
            vmem(singles.shape, f32),
            vmem((128, 128), f32),
            vmem((2, 2 * ROWS, 128), f32),
            dma((STEPS,)), dma(()), dma(()),
            dma(()), dma((STEPS, 3)), dma((N_LATE, max(LATE_STEPS), 3)),
            dma(()), dma((STEPS,)), dma((STEPS,)),
            dma((3 + 2 * N_LATE,)), dma((3 + 2 * N_LATE,)),
        ],
        compiler_params=pltpu.CompilerParams(
            collective_id=0, has_side_effects=True, vmem_limit_bytes=60 * 2**20
        ),
        cost_estimate=pl.CostEstimate(flops=2 * 3 * 256 * 256 * depth * 3, bytes_accessed=24 * 2**20, transcendentals=0),
    )(tau, integrals, singles)
    return doubles - jnp.transpose(folded, (2, 0, 1))


def solution(mesh):
    placed = (P("blk", "cd"), P("blk", "cd"), P(), P("blk", None, "cd"))
    return jax.shard_map(
        on_device, mesh=mesh, in_specs=placed, out_specs=P("blk", None, "cd"), check_vma=False
    )
```

```python
import jax
import jax.numpy as jnp
from jax import lax
from jax.experimental import pallas as pl
from jax.experimental.pallas import tpu as pltpu
from jax.sharding import PartitionSpec as P

MESH = pl.DeviceIdType.MESH
N_BLK, N_CD = 8, 16
ROWS, KA = 64, 32
LATE, N_LATE = 8, 2
EARLY = ROWS - LATE * N_LATE
STEPS = 12
LATE_STEPS = (6, 6)
OTHERS = ((1, 2), (0, 2), (0, 1))
FAR_CD = (10, 11, 6, 7, 14, 15, 8, 9, 2, 3, 4, 5, 12, 13, 1)
FAR_BLK = (6, 2, 5, 7, 4, 1, 3)
FAR_YC = (4, 5, 2, 3, 6, 7, 1)
ORDER = ((0, 1), (1, 2), (2, 1), (1, 1), (2, 2), (0, 2), (0, 3), (2, 3), (1, 3))


def corner(b):
    x = b % 4
    return (((x + 1) // 2) % 2, x // 2, b // 4)


def block_of(v):
    return v[2] * 4 + v[1] * 2 + (v[0] + v[1]) % 2


def flipped(v, dims):
    return tuple((e + 1) % 2 if at in dims else e for at, e in enumerate(v))


def masked(v, d, m):
    return flipped(v, [o for bit, o in enumerate(OTHERS[d]) if (m >> bit) & 1])


def spot(v, d):
    return v[OTHERS[d][0]] + 2 * v[OTHERS[d][1]]


def tile_at(v, d, slot):
    new = list(v)
    new[OTHERS[d][0]] = slot % 2
    new[OTHERS[d][1]] = slot // 2
    return block_of(new)


def halves(x):
    high = x.astype(jnp.bfloat16)
    return high, (x - high.astype(jnp.float32)).astype(jnp.bfloat16)


def product(a, b, stacked=False):
    def dot(l, r):
        return lax.dot_general(l, r, (((1,), (1,)), ((), ())), preferred_element_type=jnp.float32)

    if stacked:
        both = dot(jnp.concatenate(a), b[0])
        n = a[0].shape[0]
        return both[:n] + (dot(a[0], b[1]) + both[n:])
    return dot(a[0], b[0]) + (dot(a[0], b[1]) + dot(a[1], b[0]))


def arrive(ref, sem):
    pltpu.make_async_copy(ref, ref, sem).wait()


def kernel(
    tau, integrals, singles, out,
    stage, early, late, slabs, high, low, zeta, zeta_late,
    parts, summed, pieces, whole, tiles, spreads, factors, columns, spread,
    load_sem, own_sem, factor_sem, a_send, early_recv, late_recv, b_send, b_recv, f_recv, t_send, t_recv,
):
    b, c = lax.axis_index("blk"), lax.axis_index("cd")
    v = corner(b)
    depth = integrals.shape[1] // 12
    ka = depth // STEPS
    width = singles.shape[1] // N_CD
    zh, yc = c // 2 % 2, c // 4 * 2 + c % 2

    def cd_of(zh, yc):
        return yc // 2 * 4 + zh * 2 + yc % 2

    def cd_at(o):
        return (c // 4 + o // 4) % 4 * 4 + (c // 2 + o // 2) % 2 * 2 + (c + o) % 2

    def blk_at(o):
        return (b // 4 + o // 4) % 2 * 4 + (b + o) % 4

    def span(d, j, m):
        return pl.ds(pl.multiple_of((d * 4 + spot(masked(v, d, m), d)) * depth + j * ka, 128), ka)

    def send(src, dst, sent, got, blk, cd):
        pltpu.make_async_remote_copy(
            src_ref=src, dst_ref=dst, send_sem=sent, recv_sem=got, device_id=(blk, cd), device_id_type=MESH
        ).start()

    barrier = pltpu.get_barrier_semaphore()
    for o in FAR_CD:
        pl.semaphore_signal(barrier, inc=1, device_id=(b, cd_at(o)), device_id_type=MESH)
    for o in FAR_BLK:
        pl.semaphore_signal(barrier, inc=1, device_id=(blk_at(o), c), device_id_type=MESH)

    def load_start(j, carry):
        for d in range(3):
            for m in range(4):
                pltpu.make_async_copy(tau.at[:, span(d, j, m)], stage.at[j, d, m], load_sem.at[j]).start()
        return carry

    lax.fori_loop(0, STEPS, load_start, 0)
    factor_copy = pltpu.make_async_copy(singles, factors, factor_sem)
    factor_copy.start()

    def own_start(j, carry):
        for d in range(3):
            pltpu.make_async_copy(integrals.at[:, span(d, j, 0)], slabs.at[j, d, b], own_sem).start()
        return carry

    lax.fori_loop(0, STEPS, own_start, 0)

    pl.semaphore_wait(barrier, N_BLK + N_CD - 2)

    def b_start(j, carry):
        for d, m in ORDER:
            send(
                integrals.at[:, span(d, j, m)], slabs.at[j, d, b], b_send, b_recv.at[j], block_of(masked(v, d, m)), c
            )
        return carry

    lax.fori_loop(0, STEPS, b_start, 0)

    def pair_sums(j, d, m):
        back = stage[j, d, m, pl.ds(ROWS, ROWS), :].reshape(8, 8, ka)
        back = jnp.swapaxes(back, 0, 1).reshape(ROWS, ka)
        return stage[j, d, m, pl.ds(0, ROWS), :] + back

    def early_start(j, carry):
        arrive(stage.at[j], load_sem.at[j])
        for d, m in ORDER:
            stage[j, d, m, pl.ds(0, ROWS), :] = pair_sums(j, d, m)
            send(
                stage.at[j, d, m, pl.ds(0, EARLY), :], early.at[j, d, spot(v, d)],
                a_send, early_recv.at[j, d], block_of(masked(v, d, m)), c,
            )
        for d in range(3):
            sums = pair_sums(j, d, 0)
            early[j, d, spot(v, d)] = sums[:EARLY]
            for g in range(N_LATE):
                late[g, j, d, spot(v, d)] = sums[EARLY + g * LATE : EARLY + (g + 1) * LATE]
        return carry

    lax.fori_loop(0, STEPS, early_start, 0)

    arrive(slabs.at[:, :, 0], own_sem)

    def forward(j, carry):
        arrive(slabs.at[j, :, pl.ds(0, 3)], b_recv.at[j])
        for m in range(4):
            for d in range(3):
                block = slabs.at[j, d, block_of(masked(v, d, m))]
                send(block, block, b_send, f_recv.at[j], block_of(flipped(v, [d])), c)
        return carry

    lax.fori_loop(0, STEPS, forward, 0)

    def late_start(g, first, end):
        per = STEPS // LATE_STEPS[g]

        def start(n, carry):
            steps = pl.ds(n * per, per)
            for d, m in ORDER:
                send(
                    stage.at[steps, d, m, pl.ds(EARLY + g * LATE, LATE), :], late.at[g, steps, d, spot(v, d)],
                    a_send, late_recv.at[g, n, d], block_of(masked(v, d, m)), c,
                )
            return carry

        lax.fori_loop(first, end, start, 0)

    zeta[...] = jnp.zeros_like(zeta)
    zeta_late[...] = jnp.zeros_like(zeta_late)
    factor_copy.wait()
    columns[...] = pltpu.roll(factors[...], (N_CD - c) % N_CD * width, 1)[:, :128].T

    def multiply_early(j, carry):
        arrive(slabs.at[j, :, pl.ds(0, 4)], f_recv.at[j])
        for d in range(3):
            right = halves(slabs[j, d].reshape(N_BLK * KA, ka))
            high[j, d], low[j, d] = right
            arrive(early.at[j, d, pl.ds(0, 3)], early_recv.at[j, d])
            part = product(halves(early[j, d].reshape(4 * EARLY, ka)), right)
            for slot in range(4):
                t = tile_at(v, d, slot)
                rows = part[slot * EARLY : (slot + 1) * EARLY]
                for a in range(2):
                    zeta[t, a, pl.ds(0, EARLY // 8)] += rows[:, a * 128 : (a + 1) * 128].reshape(EARLY // 8, 8, 128)
        return carry

    def multiply_late(g, first, end):
        per = STEPS // LATE_STEPS[g]

        def multiply(n, carry):
            for d in range(3):
                arrive(late.at[g, pl.ds(0, per), d, pl.ds(0, 3)], late_recv.at[g, n, d])
            found = []
            for d in range(3):
                for s in range(per):
                    j = n * per + s
                    left = halves(late[g, j, d].reshape(4 * LATE, ka))
                    found.append((d, product(left, (high[j, d], low[j, d]), True)))
            for d, part in found:
                for slot in range(4):
                    t = tile_at(v, d, slot)
                    rows = part[slot * LATE : (slot + 1) * LATE]
                    for a in range(2):
                        zeta_late[g, t, a] += rows[:, a * 128 : (a + 1) * 128]
            return carry

        lax.fori_loop(first, end, multiply, 0)

    def late_to_tiles(g):
        for o in FAR_BLK:
            peer = blk_at(o)
            send(zeta_late.at[g, peer], tiles.at[g, o], t_send.at[3 + g], t_recv.at[3 + g], peer, c)

    def late_to_all(g):
        arrive(tiles.at[g, pl.ds(1, 7)], t_recv.at[3 + g])
        last = zeta_late[g, b]
        for o in range(1, N_BLK):
            last = last + tiles[g, o]
        spreads[g, c] = last
        for o in FAR_CD:
            send(
                spreads.at[g, c], spreads.at[g, c],
                t_send.at[3 + N_LATE + g], t_recv.at[3 + N_LATE + g], b, cd_at(o),
            )

    def late_rows(g):
        arrive(spreads.at[g, pl.ds(1, 15)], t_recv.at[3 + N_LATE + g])
        last = spreads[g, 0]
        for o in range(1, N_CD):
            last = last + spreads[g, o]
        at = EARLY // 8 + g
        for a in range(2):
            spread[a, pl.ds(at * 8, 8), :] = last[a]
            spread[a, pl.ds(ROWS + at, 8, stride=8), :] = last[a]

    lax.fori_loop(0, 8, multiply_early, 0)
    late_start(0, 0, 3)
    lax.fori_loop(8, 12, multiply_early, 0)
    for o in FAR_YC:
        peer = (yc // 2 + o // 2) % 4 * 2 + (yc + o) % 2
        share = zeta.at[:, peer // 4, pl.ds(peer % 4 * 2, 2)]
        send(share, parts.at[o], t_send.at[0], t_recv.at[0], b, cd_of(zh, peer))

    late_start(0, 3, 6)
    late_start(1, 0, 3)
    multiply_late(0, 0, 6)
    late_to_tiles(0)
    late_start(1, 3, 6)
    arrive(parts.at[pl.ds(1, 7)], t_recv.at[0])
    total = zeta[:, yc // 4, pl.ds(yc % 4 * 2, 2)]
    for o in range(1, 8):
        total = total + parts[o]
    summed[...] = total
    for o in FAR_BLK:
        peer = blk_at(o)
        send(summed.at[peer], pieces.at[o], t_send.at[1], t_recv.at[1], peer, c)

    multiply_late(1, 0, 6)
    late_to_tiles(1)
    late_to_all(0)
    arrive(pieces.at[pl.ds(1, 7)], t_recv.at[1])
    mine = summed[b]
    for o in range(1, N_BLK):
        mine = mine + pieces[o]
    whole[c] = mine
    for o in FAR_CD:
        send(whole.at[c], whole.at[c], t_send.at[2], t_recv.at[2], b, cd_at(o))

    late_to_all(1)
    arrive(whole.at[pl.ds(1, 15)], t_recv.at[2])
    for a in range(2):
        for i in range(EARLY // 8):
            rows = whole[cd_of(0, a * 4 + i // 2), i % 2] + whole[cd_of(1, a * 4 + i // 2), i % 2]
            spread[a, pl.ds(i * 8, 8), :] = rows
            spread[a, pl.ds(ROWS + i, 8, stride=8), :] = rows

    late_rows(0)
    arrive(slabs.at[:, :, pl.ds(0, 7)], b_send)
    arrive(early.at[:, :, pl.ds(0, 3)], a_send)
    arrive(late.at[:, :, :, pl.ds(0, 3)], a_send)
    arrive(parts.at[pl.ds(1, 7)], t_send.at[0])
    arrive(pieces.at[pl.ds(1, 7)], t_send.at[1])
    left = halves(columns[pl.ds(0, width), :])
    late_rows(1)
    for a in range(2):
        out[a] = product(left, halves(spread[a, pl.ds(0, 2 * ROWS), :]))

    arrive(whole.at[pl.ds(1, 15)], t_send.at[2])
    for g in range(N_LATE):
        arrive(tiles.at[g, pl.ds(1, 7)], t_send.at[3 + g])
        arrive(spreads.at[g, pl.ds(1, 15)], t_send.at[3 + N_LATE + g])


def on_device(integrals, tau, singles, doubles):
    depth = integrals.shape[1] // 12
    ka = depth // STEPS
    width = doubles.shape[2]
    vmem, dma, f32 = pltpu.VMEM, pltpu.SemaphoreType.DMA, jnp.float32
    any_ref, vmem_ref = pl.BlockSpec(memory_space=pl.ANY), pl.BlockSpec(memory_space=vmem)
    folded = pl.pallas_call(
        kernel,
        out_shape=jax.ShapeDtypeStruct((2, width, 2 * ROWS), f32),
        in_specs=[any_ref, any_ref, any_ref],
        out_specs=vmem_ref,
        scratch_shapes=[
            vmem((STEPS, 3, 4, 2 * ROWS, ka), f32),
            vmem((STEPS, 3, 4, EARLY, ka), f32),
            vmem((N_LATE, STEPS, 3, 4, LATE, ka), f32),
            vmem((STEPS, 3, N_BLK, KA, ka), f32),
            vmem((STEPS, 3, N_BLK * KA, ka), jnp.bfloat16),
            vmem((STEPS, 3, N_BLK * KA, ka), jnp.bfloat16),
            vmem((N_BLK, 2, 8, 8, 128), f32),
            vmem((N_LATE, N_BLK, 2, LATE, 128), f32),
            vmem((8, N_BLK, 2, 8, 128), f32),
            vmem((N_BLK, 2, 8, 128), f32),
            vmem((N_BLK, 2, 8, 128), f32),
            vmem((N_CD, 2, 8, 128), f32),
            vmem((N_LATE, N_BLK, 2, LATE, 128), f32),
            vmem((N_LATE, N_CD, 2, LATE, 128), f32),
            vmem(singles.shape, f32),
            vmem((128, 128), f32),
            vmem((2, 2 * ROWS + 8, 128), f32),
            dma((STEPS,)), dma(()), dma(()),
            dma(()), dma((STEPS, 3)), dma((N_LATE, max(LATE_STEPS), 3)),
            dma(()), dma((STEPS,)), dma((STEPS,)),
            dma((3 + 2 * N_LATE,)), dma((3 + 2 * N_LATE,)),
        ],
        compiler_params=pltpu.CompilerParams(
            collective_id=0, has_side_effects=True, vmem_limit_bytes=60 * 2**20
        ),
        cost_estimate=pl.CostEstimate(flops=2 * 3 * 256 * 256 * depth * 3, bytes_accessed=24 * 2**20, transcendentals=0),
    )(tau, integrals, singles)
    return doubles - jnp.transpose(folded, (2, 0, 1))


def solution(mesh):
    placed = (P("blk", "cd"), P("blk", "cd"), P(), P("blk", None, "cd"))
    return jax.shard_map(
        on_device, mesh=mesh, in_specs=placed, out_specs=P("blk", None, "cd"), check_vma=False
    )
```

```python
import jax
import jax.numpy as jnp
from jax import lax
from jax.experimental import pallas as pl
from jax.experimental.pallas import tpu as pltpu
from jax.sharding import PartitionSpec as P

MESH = pl.DeviceIdType.MESH
N_BLK, N_CD = 8, 16
ROWS, KA = 64, 32
LATE, N_LATE = 8, 2
EARLY = ROWS - LATE * N_LATE
SHARES = EARLY // 16
STEPS = 12
LATE_STEPS = (6, 6)
OTHERS = ((1, 2), (0, 2), (0, 1))
FAR_CD = (10, 11, 6, 7, 14, 15, 8, 9, 2, 3, 4, 5, 12, 13, 1)
FAR_BLK = (6, 2, 5, 7, 4, 1, 3)
FAR_YC = (4, 5, 2, 3, 6, 7, 1)
ORDER = ((0, 1), (1, 2), (2, 1), (1, 1), (2, 2), (0, 2), (0, 3), (2, 3), (1, 3))


def corner(b):
    x = b % 4
    return (((x + 1) // 2) % 2, x // 2, b // 4)


def block_of(v):
    return v[2] * 4 + v[1] * 2 + (v[0] + v[1]) % 2


def flipped(v, dims):
    return tuple((e + 1) % 2 if at in dims else e for at, e in enumerate(v))


def masked(v, d, m):
    return flipped(v, [o for bit, o in enumerate(OTHERS[d]) if (m >> bit) & 1])


def spot(v, d):
    return v[OTHERS[d][0]] + 2 * v[OTHERS[d][1]]


def tile_at(v, d, slot):
    new = list(v)
    new[OTHERS[d][0]] = slot % 2
    new[OTHERS[d][1]] = slot // 2
    return block_of(new)


def halves(x):
    high = x.astype(jnp.bfloat16)
    return high, (x - high.astype(jnp.float32)).astype(jnp.bfloat16)


def product(a, b, stacked=False):
    def dot(l, r):
        return lax.dot_general(l, r, (((1,), (1,)), ((), ())), preferred_element_type=jnp.float32)

    if stacked:
        both = dot(jnp.concatenate(a), b[0])
        n = a[0].shape[0]
        return both[:n] + (dot(a[0], b[1]) + both[n:])
    return dot(a[0], b[0]) + (dot(a[0], b[1]) + dot(a[1], b[0]))


def arrive(ref, sem):
    pltpu.make_async_copy(ref, ref, sem).wait()


def kernel(
    tau, integrals, singles, out,
    stage, early, late, slabs, high, low, zeta, zeta_late,
    parts, summed, pieces, whole, tiles, spreads, factors, columns, spread,
    load_sem, own_sem, factor_sem, a_send, early_recv, late_recv, b_send, b_recv, f_recv, t_send, t_recv,
):
    b, c = lax.axis_index("blk"), lax.axis_index("cd")
    v = corner(b)
    depth = integrals.shape[1] // 12
    ka = depth // STEPS
    width = singles.shape[1] // N_CD
    zh, yc = c // 2 % 2, c // 4 * 2 + c % 2

    def cd_of(zh, yc):
        return yc // 2 * 4 + zh * 2 + yc % 2

    def cd_at(o):
        return (c // 4 + o // 4) % 4 * 4 + (c // 2 + o // 2) % 2 * 2 + (c + o) % 2

    def blk_at(o):
        return (b // 4 + o // 4) % 2 * 4 + (b + o) % 4

    def span(d, j, m):
        return pl.ds(pl.multiple_of((d * 4 + spot(masked(v, d, m), d)) * depth + j * ka, 128), ka)

    def send(src, dst, sent, got, blk, cd):
        pltpu.make_async_remote_copy(
            src_ref=src, dst_ref=dst, send_sem=sent, recv_sem=got, device_id=(blk, cd), device_id_type=MESH
        ).start()

    barrier = pltpu.get_barrier_semaphore()
    for o in FAR_CD:
        pl.semaphore_signal(barrier, inc=1, device_id=(b, cd_at(o)), device_id_type=MESH)
    for o in FAR_BLK:
        pl.semaphore_signal(barrier, inc=1, device_id=(blk_at(o), c), device_id_type=MESH)

    def load_start(j, carry):
        for d in range(3):
            for m in range(4):
                pltpu.make_async_copy(tau.at[:, span(d, j, m)], stage.at[j, d, m], load_sem.at[j]).start()
        return carry

    lax.fori_loop(0, STEPS, load_start, 0)
    factor_copy = pltpu.make_async_copy(singles, factors, factor_sem)
    factor_copy.start()

    def own_start(j, carry):
        for d in range(3):
            pltpu.make_async_copy(integrals.at[:, span(d, j, 0)], slabs.at[j, d, b], own_sem).start()
        return carry

    lax.fori_loop(0, STEPS, own_start, 0)

    pl.semaphore_wait(barrier, N_BLK + N_CD - 2)

    def b_start(j, carry):
        for d, m in ORDER:
            send(
                integrals.at[:, span(d, j, m)], slabs.at[j, d, b], b_send, b_recv.at[j], block_of(masked(v, d, m)), c
            )
        return carry

    lax.fori_loop(0, STEPS, b_start, 0)

    def pair_sums(j, d, m):
        back = stage[j, d, m, pl.ds(ROWS, ROWS), :].reshape(8, 8, ka)
        back = jnp.swapaxes(back, 0, 1).reshape(ROWS, ka)
        return stage[j, d, m, pl.ds(0, ROWS), :] + back

    def early_start(j, carry):
        arrive(stage.at[j], load_sem.at[j])
        for d, m in ORDER:
            stage[j, d, m, pl.ds(0, ROWS), :] = pair_sums(j, d, m)
            send(
                stage.at[j, d, m, pl.ds(0, EARLY), :], early.at[j, d, spot(v, d)],
                a_send, early_recv.at[j, d], block_of(masked(v, d, m)), c,
            )
        for d in range(3):
            sums = pair_sums(j, d, 0)
            early[j, d, spot(v, d)] = sums[:EARLY]
            for g in range(N_LATE):
                late[g, j, d, spot(v, d)] = sums[EARLY + g * LATE : EARLY + (g + 1) * LATE]
        return carry

    lax.fori_loop(0, STEPS, early_start, 0)

    arrive(slabs.at[:, :, 0], own_sem)

    def forward(j, carry):
        arrive(slabs.at[j, :, pl.ds(0, 3)], b_recv.at[j])
        for m in range(4):
            for d in range(3):
                block = slabs.at[j, d, block_of(masked(v, d, m))]
                send(block, block, b_send, f_recv.at[j], block_of(flipped(v, [d])), c)
        return carry

    lax.fori_loop(0, STEPS, forward, 0)

    def late_start(g, first, end):
        per = STEPS // LATE_STEPS[g]

        def start(n, carry):
            steps = pl.ds(n * per, per)
            for d, m in ORDER:
                send(
                    stage.at[steps, d, m, pl.ds(EARLY + g * LATE, LATE), :], late.at[g, steps, d, spot(v, d)],
                    a_send, late_recv.at[g, n, d], block_of(masked(v, d, m)), c,
                )
            return carry

        lax.fori_loop(first, end, start, 0)

    zeta[...] = jnp.zeros_like(zeta)
    zeta_late[...] = jnp.zeros_like(zeta_late)
    factor_copy.wait()
    columns[...] = pltpu.roll(factors[...], (N_CD - c) % N_CD * width, 1)[:, :128].T

    def multiply_early(j, carry):
        arrive(slabs.at[j, :, pl.ds(0, 4)], f_recv.at[j])
        for d in range(3):
            right = halves(slabs[j, d].reshape(N_BLK * KA, ka))
            high[j, d], low[j, d] = right
            arrive(early.at[j, d, pl.ds(0, 3)], early_recv.at[j, d])
            part = product(halves(early[j, d].reshape(4 * EARLY, ka)), right)
            for slot in range(4):
                t = tile_at(v, d, slot)
                rows = part[slot * EARLY : (slot + 1) * EARLY]
                for a in range(2):
                    zeta[t, a, pl.ds(0, EARLY // 8)] += rows[:, a * 128 : (a + 1) * 128].reshape(EARLY // 8, 8, 128)
        return carry

    def multiply_late(g, first, end):
        per = STEPS // LATE_STEPS[g]

        def multiply(n, carry):
            for d in range(3):
                arrive(late.at[g, pl.ds(0, per), d, pl.ds(0, 3)], late_recv.at[g, n, d])
            found = []
            for d in range(3):
                for s in range(per):
                    j = n * per + s
                    left = halves(late[g, j, d].reshape(4 * LATE, ka))
                    found.append((d, product(left, (high[j, d], low[j, d]), True)))
            for d, part in found:
                for slot in range(4):
                    t = tile_at(v, d, slot)
                    rows = part[slot * LATE : (slot + 1) * LATE]
                    for a in range(2):
                        zeta_late[g, t, a] += rows[:, a * 128 : (a + 1) * 128]
            return carry

        lax.fori_loop(first, end, multiply, 0)

    def late_to_tiles(g):
        for o in FAR_BLK:
            peer = blk_at(o)
            send(zeta_late.at[g, peer], tiles.at[g, o], t_send.at[3 + g], t_recv.at[3 + g], peer, c)

    def late_to_all(g):
        arrive(tiles.at[g, pl.ds(1, 7)], t_recv.at[3 + g])
        last = zeta_late[g, b]
        for o in range(1, N_BLK):
            last = last + tiles[g, o]
        spreads[g, c] = last
        for o in FAR_CD:
            send(
                spreads.at[g, c], spreads.at[g, c],
                t_send.at[3 + N_LATE + g], t_recv.at[3 + N_LATE + g], b, cd_at(o),
            )

    def late_rows(g):
        arrive(spreads.at[g, pl.ds(1, 15)], t_recv.at[3 + N_LATE + g])
        last = spreads[g, 0]
        for o in range(1, N_CD):
            last = last + spreads[g, o]
        at = EARLY // 8 + g
        for a in range(2):
            spread[a, pl.ds(at * 8, 8), :] = last[a]
            spread[a, pl.ds(ROWS + at, 8, stride=8), :] = last[a]

    lax.fori_loop(0, 8, multiply_early, 0)
    late_start(0, 0, 3)
    lax.fori_loop(8, 12, multiply_early, 0)
    for o in FAR_YC:
        peer = (yc // 2 + o // 2) % 4 * 2 + (yc + o) % 2

        @pl.when(peer % 4 < SHARES)
        def _():
            share = zeta.at[:, peer // 4, pl.ds(peer % 4 * 2, 2)]
            send(share, parts.at[o], t_send.at[0], t_recv.at[0], b, cd_of(zh, peer))

    late_start(0, 3, 6)
    late_start(1, 0, 3)
    multiply_late(0, 0, 6)
    late_to_tiles(0)
    late_start(1, 3, 6)
    sharing = yc % 4 < SHARES

    @pl.when(sharing)
    def _():
        arrive(parts.at[pl.ds(1, 7)], t_recv.at[0])
        total = zeta[:, yc // 4, pl.ds(yc % 4 * 2, 2)]
        for o in range(1, 8):
            total = total + parts[o]
        summed[...] = total
        for o in FAR_BLK:
            peer = blk_at(o)
            send(summed.at[peer], pieces.at[o], t_send.at[1], t_recv.at[1], peer, c)

    multiply_late(1, 0, 6)
    late_to_tiles(1)
    late_to_all(0)

    @pl.when(sharing)
    def _():
        arrive(pieces.at[pl.ds(1, 7)], t_recv.at[1])
        mine = summed[b]
        for o in range(1, N_BLK):
            mine = mine + pieces[o]
        whole[c] = mine
        for o in FAR_CD:
            send(whole.at[c], whole.at[c], t_send.at[2], t_recv.at[2], b, cd_at(o))

    late_to_all(1)

    @pl.when(sharing)
    def _():
        arrive(whole.at[pl.ds(0, 4 * SHARES - 1)], t_recv.at[2])

    @pl.when(jnp.logical_not(sharing))
    def _():
        arrive(whole.at[pl.ds(0, 4 * SHARES)], t_recv.at[2])

    for a in range(2):
        for i in range(EARLY // 8):
            rows = whole[cd_of(0, a * 4 + i // 2), i % 2] + whole[cd_of(1, a * 4 + i // 2), i % 2]
            spread[a, pl.ds(i * 8, 8), :] = rows
            spread[a, pl.ds(ROWS + i, 8, stride=8), :] = rows

    late_rows(0)
    arrive(slabs.at[:, :, pl.ds(0, 7)], b_send)
    arrive(early.at[:, :, pl.ds(0, 3)], a_send)
    arrive(late.at[:, :, :, pl.ds(0, 3)], a_send)
    left = halves(columns[pl.ds(0, width), :])
    late_rows(1)
    for a in range(2):
        out[a] = product(left, halves(spread[a, pl.ds(0, 2 * ROWS), :]))

    @pl.when(sharing)
    def _():
        arrive(parts.at[pl.ds(0, 2 * SHARES - 1)], t_send.at[0])
        arrive(pieces.at[pl.ds(1, 7)], t_send.at[1])
        arrive(whole.at[pl.ds(1, 15)], t_send.at[2])

    @pl.when(jnp.logical_not(sharing))
    def _():
        arrive(parts.at[pl.ds(0, 2 * SHARES)], t_send.at[0])

    for g in range(N_LATE):
        arrive(tiles.at[g, pl.ds(1, 7)], t_send.at[3 + g])
        arrive(spreads.at[g, pl.ds(1, 15)], t_send.at[3 + N_LATE + g])


def on_device(integrals, tau, singles, doubles):
    depth = integrals.shape[1] // 12
    ka = depth // STEPS
    width = doubles.shape[2]
    vmem, dma, f32 = pltpu.VMEM, pltpu.SemaphoreType.DMA, jnp.float32
    any_ref, vmem_ref = pl.BlockSpec(memory_space=pl.ANY), pl.BlockSpec(memory_space=vmem)
    folded = pl.pallas_call(
        kernel,
        out_shape=jax.ShapeDtypeStruct((2, width, 2 * ROWS), f32),
        in_specs=[any_ref, any_ref, any_ref],
        out_specs=vmem_ref,
        scratch_shapes=[
            vmem((STEPS, 3, 4, 2 * ROWS, ka), f32),
            vmem((STEPS, 3, 4, EARLY, ka), f32),
            vmem((N_LATE, STEPS, 3, 4, LATE, ka), f32),
            vmem((STEPS, 3, N_BLK, KA, ka), f32),
            vmem((STEPS, 3, N_BLK * KA, ka), jnp.bfloat16),
            vmem((STEPS, 3, N_BLK * KA, ka), jnp.bfloat16),
            vmem((N_BLK, 2, 8, 8, 128), f32),
            vmem((N_LATE, N_BLK, 2, LATE, 128), f32),
            vmem((8, N_BLK, 2, 8, 128), f32),
            vmem((N_BLK, 2, 8, 128), f32),
            vmem((N_BLK, 2, 8, 128), f32),
            vmem((N_CD, 2, 8, 128), f32),
            vmem((N_LATE, N_BLK, 2, LATE, 128), f32),
            vmem((N_LATE, N_CD, 2, LATE, 128), f32),
            vmem(singles.shape, f32),
            vmem((128, 128), f32),
            vmem((2, 2 * ROWS + 8, 128), f32),
            dma((STEPS,)), dma(()), dma(()),
            dma(()), dma((STEPS, 3)), dma((N_LATE, max(LATE_STEPS), 3)),
            dma(()), dma((STEPS,)), dma((STEPS,)),
            dma((3 + 2 * N_LATE,)), dma((3 + 2 * N_LATE,)),
        ],
        compiler_params=pltpu.CompilerParams(
            collective_id=0, has_side_effects=True, vmem_limit_bytes=60 * 2**20
        ),
        cost_estimate=pl.CostEstimate(flops=2 * 3 * 256 * 256 * depth * 3, bytes_accessed=24 * 2**20, transcendentals=0),
    )(tau, integrals, singles)
    return doubles - jnp.transpose(folded, (2, 0, 1))


def solution(mesh):
    placed = (P("blk", "cd"), P("blk", "cd"), P(), P("blk", None, "cd"))
    return jax.shard_map(
        on_device, mesh=mesh, in_specs=placed, out_specs=P("blk", None, "cd"), check_vma=False
    )
```
